512 devices in a mesh: band: 8 (over y, z_hi), dom: 64 (over z_lo, x, core).
Axes of the slice: x: 4, y: 4, z: 16 (z_hi: 2, z_lo: 8; z = z_hi * 8 + z_lo), core: 2. Of those that a mesh axis runs over, the one named last changes fastest.
Arguments:
- orbitals: float32 [64, 64, 16, 16, 128], P('band', 'dom'), may hold values from -40 to 40
- potential: float32 [64, 16, 16, 128], P('dom'), may hold values from 0.2 to 4
Outputs:
- rotated: float32 [64, 64, 16, 16, 128], P('band', 'dom')
The draws below stay inside these ranges and needn't reach their ends.
All inputs are finite; a program needn't handle non-finite values.
Results may differ from the reference program's by a relative error of at most 0.0003.
Values sent between devices are 32-bit elements; how exact they have to be, the bound alone decides.
No kernel may reach another device: no remote copies, remote signals or barrier semaphores. Data moves between devices by JAX's collectives and lax.ppermute only.
A program may use at most 64 MiB of HBM per device.

```python
import math
import jax
import jax.numpy as jnp
from jax import lax

DEGREE = 4
PY = 8
CX = 16
CY = 16
NZ = 128
DOMS = 64
PX = 8
BANDS = 64
NX = 128
NY = 128


def draw_orbitals(key, part):
    key = jax.random.fold_in(key, 11)
    noise_key, shared_key, phase_key, mix_key = jax.random.split(key, 4)
    draw_shape = (BANDS, DOMS, CX, CY, NZ)
    block_ids = jnp.arange(DOMS)
    first_pos = ((block_ids // PY)[:, None] * CX + jnp.arange(CX)[None, :]).astype(jnp.float32)[:, :, None, None]
    second_pos = ((block_ids % PY)[:, None] * CY + jnp.arange(CY)[None, :]).astype(jnp.float32)[:, None, :, None]
    noise_part = jnp.clip(jax.random.normal(noise_key, draw_shape, jnp.float32), -5.0, 5.0)
    strength = 0.6
    shared = jnp.clip(jax.random.normal(shared_key, (4, DOMS, CX, CY, NZ), jnp.float32), -5.0, 5.0)
    phases = jax.random.uniform(phase_key, (4, 2), jnp.float32, 0.0, 2.0 * math.pi)
    mixing = jnp.clip(0.7 * jax.random.normal(mix_key, (BANDS, 4), jnp.float32), -2.0, 2.0)
    combined = noise_part
    for component in range(4):
        envelope = jnp.exp(strength * jnp.cos(2.0 * math.pi * first_pos / NX + phases[component, 0]) + strength * jnp.cos(2.0 * math.pi * second_pos / NY + phases[component, 1]))
        combined = combined + mixing[:, component][:, None, None, None, None] * (envelope * shared[component])[None]
    return jnp.clip(combined, -40.0, 40.0)


def level_of(rng, shape, cuts, low, top_value):
    gain = 1.0
    for position, shards_of in cuts:
        draws = jax.random.uniform(jax.random.fold_in(jax.random.fold_in(rng, 6), position), (shards_of,), jnp.float32, low / len(cuts), top_value / len(cuts))
        gain = gain * jnp.repeat(jnp.exp(draws), shape[position] // shards_of).reshape((-1,) + (1,) * (len(shape) - 1 - position))
    return gain


def setup_inputs(seed: int = 0) -> dict:
    key_of = jax.random.split(jax.random.key(seed), 3)
    orbitals = draw_orbitals(jax.random.fold_in(key_of[2], 71), 0)
    potential = jnp.clip(jnp.exp(math.log(4.0) - 2.9957323 * jax.random.uniform(key_of[1], (DOMS, CX, CY, NZ), jnp.float32) ** level_of(key_of[1], (DOMS, CX, CY, NZ), ((0, 64),), -0.2, 0.2)), 0.2, 4.0)
    return dict(orbitals=orbitals, potential=potential)


STENCIL = (-205.0 / 72.0, 8.0 / 5.0, -1.0 / 5.0, 8.0 / 315.0, -1.0 / 560.0)
FILTER_LOW = 1.5
FILTER_HIGH = 14.0

def to_grid(blocks):
    return blocks.reshape(PX, PY, CX, CY, NZ).transpose(0, 2, 1, 3, 4).reshape(PX * CX, PY * CY, NZ)

def to_blocks(grid_field):
    return grid_field.reshape(PX, CX, PY, CY, NZ).transpose(0, 2, 1, 3, 4).reshape(PX * PY, CX, CY, NZ)

def hamiltonian(grid_field, potential):
    extent = grid_field.shape
    padded = jnp.pad(grid_field, 4)
    laplace = 3.0 * STENCIL[0] * grid_field
    for axis_number in range(3):
        for shift_by in range(1, 5):
            upper_side = [slice(4, 4 + extent[0]), slice(4, 4 + extent[1]), slice(4, 4 + extent[2])]
            lower_side = list(upper_side)
            upper_side[axis_number] = slice(4 + shift_by, 4 + shift_by + extent[axis_number])
            lower_side[axis_number] = slice(4 - shift_by, 4 - shift_by + extent[axis_number])
            laplace = laplace + STENCIL[shift_by] * (padded[tuple(upper_side)] + padded[tuple(lower_side)])
    return -0.5 * laplace + potential * grid_field

def filter_band(blocks, potential_grid):
    middle = 0.5 * (FILTER_HIGH + FILTER_LOW)
    radius = 0.5 * (FILTER_HIGH - FILTER_LOW)
    grid_field = to_grid(blocks)
    earlier = grid_field
    current = (hamiltonian(grid_field, potential_grid) - middle * grid_field) / radius
    for degree_step in range(DEGREE - 1):
        following = 2.0 * (hamiltonian(current, potential_grid) - middle * current) / radius - earlier
        earlier = current
        current = following
    return to_blocks(current)

def reference(orbitals, potential):
    potential_grid = to_grid(potential)
    filtered = lax.map(lambda blocks: filter_band(blocks, potential_grid), orbitals)
    flattened = filtered.reshape(orbitals.shape[0], -1)
    cell_count = flattened.shape[1]
    gram = jnp.dot(flattened, flattened.T, precision=lax.Precision.HIGHEST) / cell_count
    factor = jnp.linalg.cholesky(gram)
    inverse = lax.linalg.triangular_solve(factor, jnp.eye(gram.shape[0], dtype=gram.dtype), left_side=True, lower=True)
    rotated = jnp.dot(inverse, flattened, precision=lax.Precision.HIGHEST)
    return rotated.reshape(orbitals.shape)
```

```python
import jax
import jax.numpy as jnp
from jax import lax
from jax.sharding import PartitionSpec as P

DEGREE = 4
PY = 8


STENCIL = (-205.0 / 72.0, 8.0 / 5.0, -1.0 / 5.0, 8.0 / 315.0, -1.0 / 560.0)
FILTER_LOW = 1.5
FILTER_HIGH = 14.0


def from_behind(block, axis, distance):
    devices = range(lax.axis_size(axis))
    route = [(i - distance, i) for i in devices if i - distance in devices]
    return lax.ppermute(block, axis, route)


def from_neighbour(rim, offset):
    return from_behind(rim, "dom", offset)


def hamiltonian(grid_field, potential, keep_low, keep_high):
    plane_count = grid_field.shape[1]
    row_count = grid_field.shape[2]
    layer_count = grid_field.shape[3]
    lower_rim = from_neighbour(grid_field[:, plane_count - 4 :], PY)
    upper_rim = from_neighbour(grid_field[:, :4], -PY)
    front_rim = from_neighbour(grid_field[:, :, row_count - 4 :], 1) * keep_low
    back_rim = from_neighbour(grid_field[:, :, :4], -1) * keep_high
    first_padded = jnp.concatenate((lower_rim, grid_field, upper_rim), axis=1)
    second_padded = jnp.concatenate((front_rim, grid_field, back_rim), axis=2)
    third_padded = jnp.pad(grid_field, ((0, 0), (0, 0), (0, 0), (4, 4)))
    laplace = 3.0 * STENCIL[0] * grid_field
    for shift_by in range(1, 5):
        laplace = laplace + STENCIL[shift_by] * (
            first_padded[:, 4 + shift_by : 4 + shift_by + plane_count]
            + first_padded[:, 4 - shift_by : 4 - shift_by + plane_count]
        )
        laplace = laplace + STENCIL[shift_by] * (
            second_padded[:, :, 4 + shift_by : 4 + shift_by + row_count]
            + second_padded[:, :, 4 - shift_by : 4 - shift_by + row_count]
        )
        laplace = laplace + STENCIL[shift_by] * (
            third_padded[:, :, :, 4 + shift_by : 4 + shift_by + layer_count]
            + third_padded[:, :, :, 4 - shift_by : 4 - shift_by + layer_count]
        )
    return -0.5 * laplace + potential[None] * grid_field


def orthonormal(gram):
    factor = jnp.linalg.cholesky(gram)
    return lax.linalg.triangular_solve(
        factor, jnp.eye(gram.shape[0], dtype=gram.dtype), left_side=True, lower=True
    )


def spread(row, axis):
    copies = jnp.broadcast_to(row[None], (lax.axis_size(axis),) + row.shape)
    return lax.all_to_all(copies, axis, 0, 0, tiled=True)


def summed_everywhere(gram):
    row = lax.all_to_all(gram[:, None], "dom", 0, 0, tiled=True).sum(axis=0)
    row = spread(row, "band").sum(axis=0)
    return spread(row, "dom")[:, 0]


def on_device(orbitals, potential):
    local_orbitals = orbitals[:, 0]
    local_potential = potential[0]
    column_index = lax.axis_index("dom") % PY
    keep_low = (column_index != 0).astype(jnp.float32)
    keep_high = (column_index != PY - 1).astype(jnp.float32)
    middle = 0.5 * (FILTER_HIGH + FILTER_LOW)
    radius = 0.5 * (FILTER_HIGH - FILTER_LOW)
    earlier = local_orbitals
    current = (
        hamiltonian(local_orbitals, local_potential, keep_low, keep_high) - middle * local_orbitals
    ) / radius
    for degree_step in range(DEGREE - 1):
        following = (
            2.0
            * (hamiltonian(current, local_potential, keep_low, keep_high) - middle * current)
            / radius
            - earlier
        )
        earlier = current
        current = following
    cell_count = (
        local_orbitals.shape[1]
        * local_orbitals.shape[2]
        * local_orbitals.shape[3]
        * lax.axis_size("dom")
    )
    layers = local_orbitals.shape[3]
    rows = current.reshape(local_orbitals.shape[0], -1, layers)
    share = lax.all_to_all(rows, "band", 1, 0, tiled=True)
    bands = share.shape[0]
    share = share.reshape(bands, -1)
    gram = summed_everywhere(jnp.dot(share, share.T, precision=lax.Precision.HIGHEST))
    inverse = orthonormal(gram / cell_count)
    rotated = jnp.dot(inverse, share, precision=lax.Precision.HIGHEST)
    rotated = lax.all_to_all(rotated.reshape(bands, -1, layers), "band", 0, 1, tiled=True)
    return rotated.reshape(orbitals.shape)


def solution(mesh):
    placed = (P("band", "dom", None, None, None), P("dom", None, None, None))
    return jax.shard_map(
        on_device,
        mesh=mesh,
        in_specs=placed,
        out_specs=P("band", "dom", None, None, None),
        check_vma=False,
    )
```

```python
import jax
import jax.numpy as jnp
from jax import lax
from jax.sharding import PartitionSpec as P

DEGREE = 4
PY = 8


STENCIL = (-205.0 / 72.0, 8.0 / 5.0, -1.0 / 5.0, 8.0 / 315.0, -1.0 / 560.0)
FILTER_LOW = 1.5
FILTER_HIGH = 14.0


def from_behind(block, axis, distance):
    devices = range(lax.axis_size(axis))
    route = [(i - distance, i) for i in devices if i - distance in devices]
    return lax.ppermute(block, axis, route)


def from_neighbour(rim, offset):
    return from_behind(rim, "dom", offset)


def hamiltonian(grid_field, potential, keep_low, keep_high):
    plane_count = grid_field.shape[1]
    row_count = grid_field.shape[2]
    layer_count = grid_field.shape[3]
    lower_rim = from_neighbour(grid_field[:, plane_count - 4 :], PY)
    upper_rim = from_neighbour(grid_field[:, :4], -PY)
    front_rim = from_neighbour(grid_field[:, :, row_count - 4 :], 1) * keep_low
    back_rim = from_neighbour(grid_field[:, :, :4], -1) * keep_high
    first_padded = jnp.concatenate((lower_rim, grid_field, upper_rim), axis=1)
    second_padded = jnp.concatenate((front_rim, grid_field, back_rim), axis=2)
    third_padded = jnp.pad(grid_field, ((0, 0), (0, 0), (0, 0), (4, 4)))
    laplace = 3.0 * STENCIL[0] * grid_field
    for shift_by in range(1, 5):
        laplace = laplace + STENCIL[shift_by] * (
            first_padded[:, 4 + shift_by : 4 + shift_by + plane_count]
            + first_padded[:, 4 - shift_by : 4 - shift_by + plane_count]
        )
        laplace = laplace + STENCIL[shift_by] * (
            second_padded[:, :, 4 + shift_by : 4 + shift_by + row_count]
            + second_padded[:, :, 4 - shift_by : 4 - shift_by + row_count]
        )
        laplace = laplace + STENCIL[shift_by] * (
            third_padded[:, :, :, 4 + shift_by : 4 + shift_by + layer_count]
            + third_padded[:, :, :, 4 - shift_by : 4 - shift_by + layer_count]
        )
    return -0.5 * laplace + potential[None] * grid_field


def orthonormal(gram):
    factor = jnp.linalg.cholesky(gram)
    return lax.linalg.triangular_solve(
        factor, jnp.eye(gram.shape[0], dtype=gram.dtype), left_side=True, lower=True
    )


def member(y, z_hi, z_lo, plane):
    return (y * 2 + z_hi) * 64 + z_lo * 8 + plane


Y_RINGS = [[0, 2, 4, 6], [1, 3, 5, 7]]
SHEETS = [
    [member(y, z_hi, z_lo, plane) for y in range(4) for plane in range(8)]
    for z_hi in range(2)
    for z_lo in range(8)
]
Z_RINGS = [
    [member(y, z_hi, z_lo, plane) for z_hi in range(2) for z_lo in range(8)]
    for y in range(4)
    for plane in range(8)
]


def over_y(block, split, joined):
    return lax.all_to_all(block, "band", split, joined, axis_index_groups=Y_RINGS, tiled=True)


def across(block):
    return lax.ppermute(block, "band", [(i, i ^ 1) for i in range(8)])


def small_exchange(chunks, groups):
    return lax.all_to_all(chunks, ("band", "dom"), 0, 0, axis_index_groups=groups, tiled=True)


def spread(row, groups):
    count = len(groups[0])
    return small_exchange(jnp.broadcast_to(row, (count,) + row.shape[1:]), groups)


def summed_everywhere(gram):
    row = small_exchange(gram.reshape(32, 1, 128), SHEETS).sum(axis=0, keepdims=True)
    row = spread(row, Z_RINGS).sum(axis=0, keepdims=True)
    return spread(row, SHEETS).reshape(gram.shape)


def own_first(matrix, side):
    size = matrix.shape[0] // 2
    return jnp.where(side == 0, matrix, jnp.roll(matrix, (size, size), (0, 1)))


def by_group(matrix):
    return matrix.reshape(2, 4, 8, 2, 4, 8).transpose(1, 0, 2, 4, 3, 5).reshape(64, 64)


def by_side(matrix):
    return matrix.reshape(4, 2, 8, 4, 2, 8).transpose(1, 0, 2, 4, 3, 5).reshape(64, 64)


def on_device(orbitals, potential):
    local_orbitals = orbitals[:, 0]
    local_potential = potential[0]
    column_index = lax.axis_index("dom") % PY
    keep_low = (column_index != 0).astype(jnp.float32)
    keep_high = (column_index != PY - 1).astype(jnp.float32)
    middle = 0.5 * (FILTER_HIGH + FILTER_LOW)
    radius = 0.5 * (FILTER_HIGH - FILTER_LOW)
    earlier = local_orbitals
    current = (
        hamiltonian(local_orbitals, local_potential, keep_low, keep_high) - middle * local_orbitals
    ) / radius
    for degree_step in range(DEGREE - 1):
        following = (
            2.0
            * (hamiltonian(current, local_potential, keep_low, keep_high) - middle * current)
            / radius
            - earlier
        )
        earlier = current
        current = following
    cell_count = (
        local_orbitals.shape[1]
        * local_orbitals.shape[2]
        * local_orbitals.shape[3]
        * lax.axis_size("dom")
    )
    layers = local_orbitals.shape[3]
    rows = current.reshape(local_orbitals.shape[0], -1, layers)
    side = lax.axis_index("band") % 2
    share = over_y(rows, 1, 0)
    half = share.shape[1] // 2
    kept = lax.dynamic_slice_in_dim(share, side * half, half, 1)
    given = lax.dynamic_slice_in_dim(share, (1 - side) * half, half, 1)
    taken = across(given)
    kept_late, taken = lax.optimization_barrier((kept, taken))
    taken_late = across(kept_late)
    count = share.shape[0]
    both = jnp.concatenate((kept, taken)).reshape(2 * count, -1)
    gram = jnp.dot(both, both.T, precision=lax.Precision.HIGHEST)
    gram = summed_everywhere(own_first(gram, side)) / cell_count
    inverse = orthonormal(by_group(gram))
    inverse = own_first(by_side(inverse), side)[:count]
    late = jnp.concatenate((given, taken_late)).reshape(2 * count, -1)
    early_out = jnp.dot(inverse, both, precision=lax.Precision.HIGHEST).reshape(count, half, layers)
    late_out = jnp.dot(inverse, late, precision=lax.Precision.HIGHEST).reshape(count, half, layers)
    first = jnp.where(side == 0, early_out, late_out)
    second = jnp.where(side == 0, late_out, early_out)
    rotated = over_y(jnp.concatenate((first, second), axis=1), 0, 1)
    return rotated.reshape(orbitals.shape)


def solution(mesh):
    placed = (P("band", "dom", None, None, None), P("dom", None, None, None))
    return jax.shard_map(
        on_device,
        mesh=mesh,
        in_specs=placed,
        out_specs=P("band", "dom", None, None, None),
        check_vma=False,
    )
```

```python
import functools

import jax
import jax.numpy as jnp
import numpy as np
from jax import lax
from jax.experimental import pallas as pl
from jax.experimental.pallas import tpu as pltpu
from jax.sharding import PartitionSpec as P

STENCIL = (-205.0 / 72.0, 8.0 / 5.0, -1.0 / 5.0, 8.0 / 315.0, -1.0 / 560.0)
FILTER_LOW = 1.5
FILTER_HIGH = 14.0
MIDDLE = 0.5 * (FILTER_HIGH + FILTER_LOW)
RADIUS = 0.5 * (FILTER_HIGH - FILTER_LOW)
SIDE_STEP = tuple(-0.5 * c / RADIUS for c in STENCIL)

PX = 8
PY = 8
CX = 16
CY = 16
NZ = 128
GROUP = 8
REACH = 4
DEEP = 8
VMEM_BYTES = 40 * 2**20


def member(y, z_hi, z_lo, plane):
    return (y * 2 + z_hi) * 64 + z_lo * 8 + plane


Y_RINGS = [[0, 2, 4, 6], [1, 3, 5, 7]]
Z_PAIRS = [[0, 1], [2, 3], [4, 5], [6, 7]]
SHEETS = [
    [member(y, z_hi, z_lo, plane) for y in range(4) for plane in range(8)]
    for z_hi in range(2)
    for z_lo in range(8)
]
Z_RINGS = [
    [member(y, z_hi, z_lo, plane) for z_hi in range(2) for z_lo in range(8)]
    for y in range(4)
    for plane in range(8)
]


def third_dimension_matrix():
    matrix = np.zeros((NZ, NZ))
    for offset in range(1, REACH + 1):
        band = np.eye(NZ, k=offset) + np.eye(NZ, k=-offset)
        matrix += SIDE_STEP[offset] * band
    matrix += np.eye(NZ) * (3.0 * SIDE_STEP[0] - MIDDLE / RADIUS)
    return matrix.astype(np.float32)


def scaled_hamiltonian(field, potential, along, plane, first, count, origin):
    here = field[plane, pl.ds(first, count)]
    total = jnp.dot(
        here.reshape(count * GROUP, NZ),
        along[...],
        precision=lax.Precision.HIGHEST,
        preferred_element_type=jnp.float32,
    ).reshape(count, GROUP, NZ)
    for offset in range(1, REACH + 1):
        total += SIDE_STEP[offset] * (
            (field[plane + offset, pl.ds(first, count)] + field[plane - offset, pl.ds(first, count)])
            + (
                field[plane, pl.ds(first + offset, count)]
                + field[plane, pl.ds(first - offset, count)]
            )
        )
    local = potential[plane - origin, pl.ds(first - origin, count)] * (1.0 / RADIUS)
    return total + local[:, None, :] * here


def rims_kernel(field, potential, low, high, front, back):
    low[: DEEP * CY] = field[:DEEP].reshape(DEEP * CY, GROUP, NZ)
    high[: DEEP * CY] = field[CX - DEEP :].reshape(DEEP * CY, GROUP, NZ)
    front[: CX * DEEP] = field[:, :DEEP].reshape(CX * DEEP, GROUP, NZ)
    back[: CX * DEEP] = field[:, CY - DEEP :].reshape(CX * DEEP, GROUP, NZ)
    if potential is not None:
        tail = DEEP * CY
        low[tail:] = potential[:REACH].reshape(8, 8, NZ)
        high[tail:] = potential[CX - REACH :].reshape(8, 8, NZ)
        for plane in range(CX):
            slot, row = tail + plane // 2, plane % 2 * REACH
            front[slot, row : row + REACH] = potential[plane, :REACH]
            back[slot, row : row + REACH] = potential[plane, CY - REACH :]


def fill_padded(padded, field, low, high, front, back, low_corner, high_corner):
    end = DEEP + CX
    padded[DEEP:end, DEEP:end] = field[...]
    padded[:DEEP, DEEP:end] = low[: DEEP * CY].reshape(DEEP, CY, GROUP, NZ)
    padded[end:, DEEP:end] = high[: DEEP * CY].reshape(DEEP, CY, GROUP, NZ)
    padded[DEEP:end, :DEEP] = front[: CX * DEEP].reshape(CX, DEEP, GROUP, NZ)
    padded[DEEP:end, end:] = back[: CX * DEEP].reshape(CX, DEEP, GROUP, NZ)
    for rows, corner in ((DEEP - REACH, low_corner), (end, high_corner)):
        padded[rows : rows + REACH, DEEP - REACH : DEEP] = corner[:, :REACH]
        padded[rows : rows + REACH, end : end + REACH] = corner[:, REACH:]


def kept_sides():
    place = lax.axis_index("dom")
    row, column = place // PY, place % PY
    return tuple(
        jnp.where(edge, 0.0, 1.0)
        for edge in (row == 0, row == PX - 1, column == 0, column == PY - 1)
    )


def wide_step(padded, potential, along, earlier, later):
    keep_low, keep_high, keep_front, keep_back = kept_sides()

    def value(plane, first, count):
        total = scaled_hamiltonian(padded, potential, along, plane + DEEP, first + DEEP, count, REACH)
        if earlier is not None:
            total = 2.0 * total - earlier[plane + REACH, pl.ds(first + REACH, count)]
        return total

    def middle(plane, carry):
        total = value(plane, -REACH, CY + 2 * REACH)
        later[plane + REACH, :REACH] = total[:REACH] * keep_front
        later[plane + REACH, REACH : REACH + CY] = total[REACH : REACH + CY]
        later[plane + REACH, REACH + CY :] = total[REACH + CY :] * keep_back
        return carry

    def outer(layer, carry):
        later[layer, REACH : REACH + CY] = value(layer - REACH, 0, CY) * keep_low
        later[layer + CX + REACH, REACH : REACH + CY] = value(layer + CX, 0, CY) * keep_high
        return carry

    lax.fori_loop(0, CX, middle, 0)
    lax.fori_loop(0, REACH, outer, 0)


def narrow_step(wide, potential, along, earlier, store):
    def body(plane, carry):
        total = scaled_hamiltonian(wide, potential, along, plane + REACH, REACH, CY, 0)
        store(plane, 2.0 * total - earlier[plane])
        return carry

    lax.fori_loop(0, CX, body, 0)


def first_pair_kernel(
    field, potential, low, high, front, back, low_corner, high_corner, along,
    once, twice, wide_potential, next_low, next_high, next_front, next_back, padded,
):
    fill_padded(padded, field, low, high, front, back, low_corner, high_corner)
    tail, end = DEEP * CY, REACH + CX
    wide_potential[...] = jnp.zeros_like(wide_potential)
    wide_potential[REACH:end, REACH:end] = potential[...]
    wide_potential[:REACH, REACH:end] = low[tail:].reshape(REACH, CY, NZ)
    wide_potential[end:, REACH:end] = high[tail:].reshape(REACH, CY, NZ)
    for plane in range(CX):
        slot, row = tail + plane // 2, plane % 2 * REACH
        wide_potential[REACH + plane, :REACH] = front[slot, row : row + REACH]
        wide_potential[REACH + plane, end:] = back[slot, row : row + REACH]
    wide_step(padded, wide_potential, along, None, once)

    def store(plane, total):
        twice[plane] = total

    narrow_step(once, wide_potential, along, field, store)
    rims_kernel(twice, None, next_low, next_high, next_front, next_back)


def second_pair_kernel(
    field, once, potential, low, high, front, back, low_corner, high_corner, along,
    given, kept, padded, wide,
):
    fill_padded(padded, field, low, high, front, back, low_corner, high_corner)
    wide_step(padded, potential, along, once, wide)
    side = lax.axis_index("band") % 2

    def store(plane, total):
        row = pl.multiple_of((plane // 4 * 2 + plane % 2) * CY, CY)
        mine = plane // 2 % 2 == side

        @pl.when(mine)
        def _():
            kept[pl.ds(row, CY)] = total

        @pl.when(jnp.logical_not(mine))
        def _():
            given[pl.ds(row, CY)] = total

    narrow_step(wide, potential, along, field, store)


def call(kernel, shapes, scratch, *operands):
    whole = pl.BlockSpec(memory_space=pltpu.VMEM)
    return pl.pallas_call(
        kernel,
        out_shape=[jax.ShapeDtypeStruct(shape, jnp.float32) for shape in shapes],
        in_specs=[whole] * len(operands),
        out_specs=[whole] * len(shapes),
        scratch_shapes=[pltpu.VMEM(shape, jnp.float32) for shape in scratch],
        compiler_params=pltpu.CompilerParams(vmem_limit_bytes=VMEM_BYTES),
    )(*operands)


def along_rows(rim, offset):
    route = [(i - offset * PY, i) for i in range(PX * PY) if 0 <= i // PY - offset < PX]
    return lax.ppermute(rim, "dom", route)


def along_columns(rim, offset):
    route = [(i - offset, i) for i in range(PX * PY) if 0 <= i % PY - offset < PY]
    return lax.ppermute(rim, "dom", route)


def halo(low, high, front, back):
    from_low, from_high = along_rows(high, 1), along_rows(low, -1)
    from_front, from_back = along_columns(back, 1), along_columns(front, -1)
    side_shape = (CX, DEEP, GROUP, NZ)
    front_side = from_front[: CX * DEEP].reshape(side_shape)
    back_side = from_back[: CX * DEEP].reshape(side_shape)

    def corners(planes):
        return jnp.concatenate(
            (front_side[planes, DEEP - REACH :], back_side[planes, :REACH]), axis=1
        )

    low_corner = along_rows(corners(slice(CX - REACH, CX)), 1)
    high_corner = along_rows(corners(slice(0, REACH)), -1)
    return from_low, from_high, from_front, from_back, low_corner, high_corner


def filtered_halves(orbitals, potential):
    field = orbitals.transpose(1, 2, 0, 3)
    along = jnp.asarray(third_dimension_matrix())
    tiles = DEEP * CY
    block = (CX, CY, GROUP, NZ)
    wide = (CX + 2 * REACH, CY + 2 * REACH, GROUP, NZ)
    padded = (CX + 2 * DEEP, CY + 2 * DEEP, GROUP, NZ)
    rims = call(rims_kernel, [(tiles + 8, GROUP, NZ)] * 4, [], field, potential)
    once, twice, wide_potential, *rims = call(
        first_pair_kernel,
        [wide, block, wide[:2] + (NZ,)] + [(tiles, GROUP, NZ)] * 4,
        [padded],
        field, potential, *halo(*rims), along,
    )
    return call(
        second_pair_kernel,
        [(tiles, GROUP, NZ)] * 2,
        [padded, wide],
        twice, once, wide_potential, *halo(*rims), along,
    )


def over_y(block):
    return lax.all_to_all(block, "band", 0, 0, axis_index_groups=Y_RINGS, tiled=True)


def across(block):
    return lax.ppermute(block, "band", [(i, i ^ 1) for i in range(8)])


def small_exchange(chunks, groups):
    return lax.all_to_all(chunks, ("band", "dom"), 0, 0, axis_index_groups=groups, tiled=True)


def spread(row, groups):
    count = len(groups[0])
    return small_exchange(jnp.broadcast_to(row, (count,) + row.shape[1:]), groups)


def summed_everywhere(gram):
    row = small_exchange(gram.reshape(32, 1, 128), SHEETS).sum(axis=0, keepdims=True)
    row = spread(row, Z_RINGS).sum(axis=0, keepdims=True)
    return spread(row, SHEETS).reshape(gram.shape)


def own_first(matrix, side):
    size = matrix.shape[0] // 2
    return jnp.where(side == 0, matrix, jnp.roll(matrix, (size, size), (0, 1)))


def by_group(matrix):
    return matrix.reshape(2, 4, 8, 2, 4, 8).transpose(1, 0, 2, 4, 3, 5).reshape(64, 64)


def by_side(matrix):
    return matrix.reshape(4, 2, 8, 4, 2, 8).transpose(1, 0, 2, 4, 3, 5).reshape(64, 64)


def orthonormal(gram):
    factor = jnp.linalg.cholesky(gram)
    return lax.linalg.triangular_solve(
        factor, jnp.eye(gram.shape[0], dtype=gram.dtype), left_side=True, lower=True
    )


def bands_by_rows(block):
    rows = block.shape[0] // 4
    return block.reshape(4, rows, GROUP, NZ).transpose(0, 2, 1, 3).reshape(4 * GROUP, rows, NZ)


def on_device(orbitals, potential):
    cell_count = CX * CY * NZ * lax.axis_size("dom")
    given, kept = filtered_halves(orbitals[:, 0], potential[0])
    side = lax.axis_index("band") % 2
    given = over_y(given)
    taken = across(given)
    kept = over_y(kept)
    kept_late, taken = lax.optimization_barrier((kept, taken))
    late_pair = lax.all_gather(kept_late, "band", axis=0, axis_index_groups=Z_PAIRS)
    taken_late = jnp.where(side == 0, late_pair[1], late_pair[0])
    count, half = 32, 32
    both = jnp.concatenate((bands_by_rows(kept), bands_by_rows(taken))).reshape(2 * count, -1)
    gram = jnp.dot(both, both.T, precision=lax.Precision.HIGHEST)
    gram = summed_everywhere(own_first(gram, side)) / cell_count
    inverse = orthonormal(by_group(gram))
    inverse = own_first(by_side(inverse), side)[:count]
    late = jnp.concatenate((bands_by_rows(given), bands_by_rows(taken_late))).reshape(2 * count, -1)
    early_out = jnp.dot(inverse, both, precision=lax.Precision.HIGHEST).reshape(count, half, NZ)
    late_out = jnp.dot(inverse, late, precision=lax.Precision.HIGHEST).reshape(count, half, NZ)
    first = jnp.where(side == 0, early_out, late_out)
    second = jnp.where(side == 0, late_out, early_out)
    rotated = lax.all_to_all(
        jnp.concatenate((first, second), axis=1), "band", 0, 1, axis_index_groups=Y_RINGS, tiled=True
    )
    return rotated.reshape(orbitals.shape)


def solution(mesh):
    placed = (P("band", "dom", None, None, None), P("dom", None, None, None))
    return jax.shard_map(
        on_device,
        mesh=mesh,
        in_specs=placed,
        out_specs=P("band", "dom", None, None, None),
        check_vma=False,
    )
```

```python
import functools

import functools

import jax
import jax.numpy as jnp
import numpy as np
from jax import lax
from jax.experimental import pallas as pl
from jax.experimental.pallas import tpu as pltpu
from jax.sharding import PartitionSpec as P

STENCIL = (-205.0 / 72.0, 8.0 / 5.0, -1.0 / 5.0, 8.0 / 315.0, -1.0 / 560.0)
FILTER_LOW = 1.5
FILTER_HIGH = 14.0
MIDDLE = 0.5 * (FILTER_HIGH + FILTER_LOW)
RADIUS = 0.5 * (FILTER_HIGH - FILTER_LOW)
SIDE_STEP = tuple(-0.5 * c / RADIUS for c in STENCIL)

PX = 8
PY = 8
CX = 16
CY = 16
NZ = 128
GROUP = 8
REACH = 4
DEEP = 8
BANDS = 64
HALF = 32
VMEM_BYTES = 40 * 2**20


def member(y, z_hi, z_lo, plane):
    return (y * 2 + z_hi) * 64 + z_lo * 8 + plane


Y_RINGS = [[0, 2, 4, 6], [1, 3, 5, 7]]
SHEETS = [
    [member(y, z_hi, z_lo, plane) for y in range(4) for plane in range(8)]
    for z_hi in range(2)
    for z_lo in range(8)
]
Z_RINGS = [
    [member(y, z_hi, z_lo, plane) for z_hi in range(2) for z_lo in range(8)]
    for y in range(4)
    for plane in range(8)
]


def third_dimension_matrix():
    matrix = np.zeros((NZ, NZ))
    for offset in range(1, REACH + 1):
        band = np.eye(NZ, k=offset) + np.eye(NZ, k=-offset)
        matrix += SIDE_STEP[offset] * band
    matrix += np.eye(NZ) * (3.0 * SIDE_STEP[0] - MIDDLE / RADIUS)
    return matrix.astype(np.float32)


def scaled_hamiltonian(field, potential, along, plane, first, count, origin):
    here = field[plane, pl.ds(first, count)]
    total = jnp.dot(
        here.reshape(count * GROUP, NZ),
        along[...],
        precision=lax.Precision.HIGHEST,
        preferred_element_type=jnp.float32,
    ).reshape(count, GROUP, NZ)
    for offset in range(1, REACH + 1):
        total += SIDE_STEP[offset] * (
            (field[plane + offset, pl.ds(first, count)] + field[plane - offset, pl.ds(first, count)])
            + (
                field[plane, pl.ds(first + offset, count)]
                + field[plane, pl.ds(first - offset, count)]
            )
        )
    local = potential[plane - origin, pl.ds(first - origin, count)] * (1.0 / RADIUS)
    return total + local[:, None, :] * here


def rims_kernel(field, potential, low, high, front, back):
    low[: DEEP * CY] = field[:DEEP].reshape(DEEP * CY, GROUP, NZ)
    high[: DEEP * CY] = field[CX - DEEP :].reshape(DEEP * CY, GROUP, NZ)
    front[: CX * DEEP] = field[:, :DEEP].reshape(CX * DEEP, GROUP, NZ)
    back[: CX * DEEP] = field[:, CY - DEEP :].reshape(CX * DEEP, GROUP, NZ)
    if potential is not None:
        tail = DEEP * CY
        low[tail:] = potential[:REACH].reshape(8, 8, NZ)
        high[tail:] = potential[CX - REACH :].reshape(8, 8, NZ)
        for plane in range(CX):
            slot, row = tail + plane // 2, plane % 2 * REACH
            front[slot, row : row + REACH] = potential[plane, :REACH]
            back[slot, row : row + REACH] = potential[plane, CY - REACH :]


def fill_padded(padded, field, low, high, front, back, low_corner, high_corner):
    end = DEEP + CX
    padded[DEEP:end, DEEP:end] = field[...]
    padded[:DEEP, DEEP:end] = low[: DEEP * CY].reshape(DEEP, CY, GROUP, NZ)
    padded[end:, DEEP:end] = high[: DEEP * CY].reshape(DEEP, CY, GROUP, NZ)
    padded[DEEP:end, :DEEP] = front[: CX * DEEP].reshape(CX, DEEP, GROUP, NZ)
    padded[DEEP:end, end:] = back[: CX * DEEP].reshape(CX, DEEP, GROUP, NZ)
    for rows, corner in ((DEEP - REACH, low_corner), (end, high_corner)):
        padded[rows : rows + REACH, DEEP - REACH : DEEP] = corner[:, :REACH]
        padded[rows : rows + REACH, end : end + REACH] = corner[:, REACH:]


def kept_sides():
    place = lax.axis_index("dom")
    row, column = place // PY, place % PY
    return tuple(
        jnp.where(edge, 0.0, 1.0)
        for edge in (row == 0, row == PX - 1, column == 0, column == PY - 1)
    )


def wide_step(padded, potential, along, earlier, later):
    keep_low, keep_high, keep_front, keep_back = kept_sides()

    def value(plane, first, count):
        total = scaled_hamiltonian(padded, potential, along, plane + DEEP, first + DEEP, count, REACH)
        if earlier is not None:
            total = 2.0 * total - earlier[plane + REACH, pl.ds(first + REACH, count)]
        return total

    def middle(plane, carry):
        total = value(plane, -REACH, CY + 2 * REACH)
        later[plane + REACH, :REACH] = total[:REACH] * keep_front
        later[plane + REACH, REACH : REACH + CY] = total[REACH : REACH + CY]
        later[plane + REACH, REACH + CY :] = total[REACH + CY :] * keep_back
        return carry

    def outer(layer, carry):
        later[layer, REACH : REACH + CY] = value(layer - REACH, 0, CY) * keep_low
        later[layer + CX + REACH, REACH : REACH + CY] = value(layer + CX, 0, CY) * keep_high
        return carry

    lax.fori_loop(0, CX, middle, 0)
    lax.fori_loop(0, REACH, outer, 0)


def narrow_step(wide, potential, along, earlier, store):
    def body(plane, carry):
        total = scaled_hamiltonian(wide, potential, along, plane + REACH, REACH, CY, 0)
        store(plane, 2.0 * total - earlier[plane])
        return carry

    lax.fori_loop(0, CX, body, 0)


def first_pair_kernel(
    field, potential, low, high, front, back, low_corner, high_corner, along,
    once, twice, wide_potential, next_low, next_high, next_front, next_back, padded,
):
    fill_padded(padded, field, low, high, front, back, low_corner, high_corner)
    tail, end = DEEP * CY, REACH + CX
    wide_potential[...] = jnp.zeros_like(wide_potential)
    wide_potential[REACH:end, REACH:end] = potential[...]
    wide_potential[:REACH, REACH:end] = low[tail:].reshape(REACH, CY, NZ)
    wide_potential[end:, REACH:end] = high[tail:].reshape(REACH, CY, NZ)
    for plane in range(CX):
        slot, row = tail + plane // 2, plane % 2 * REACH
        wide_potential[REACH + plane, :REACH] = front[slot, row : row + REACH]
        wide_potential[REACH + plane, end:] = back[slot, row : row + REACH]
    wide_step(padded, wide_potential, along, None, once)

    def store(plane, total):
        twice[plane] = total

    narrow_step(once, wide_potential, along, field, store)
    rims_kernel(twice, None, next_low, next_high, next_front, next_back)


def second_pair_kernel(
    field, once, potential, low, high, front, back, low_corner, high_corner, along,
    given, kept, padded, wide,
):
    fill_padded(padded, field, low, high, front, back, low_corner, high_corner)
    wide_step(padded, potential, along, once, wide)
    side = lax.axis_index("band") % 2

    def store(plane, total):
        row = pl.multiple_of((plane // 4 * 2 + plane % 2) * CY, CY)
        mine = plane // 2 % 2 == side

        @pl.when(mine)
        def _():
            kept[pl.ds(row, CY)] = total

        @pl.when(jnp.logical_not(mine))
        def _():
            given[pl.ds(row, CY)] = total

    narrow_step(wide, potential, along, field, store)


def call(kernel, shapes, scratch, *operands):
    whole = pl.BlockSpec(memory_space=pltpu.VMEM)
    return pl.pallas_call(
        kernel,
        out_shape=[jax.ShapeDtypeStruct(shape, jnp.float32) for shape in shapes],
        in_specs=[whole] * len(operands),
        out_specs=[whole] * len(shapes),
        scratch_shapes=[pltpu.VMEM(shape, jnp.float32) for shape in scratch],
        compiler_params=pltpu.CompilerParams(vmem_limit_bytes=VMEM_BYTES),
    )(*operands)


def along_rows(rim, offset):
    route = [(i - offset * PY, i) for i in range(PX * PY) if 0 <= i // PY - offset < PX]
    return lax.ppermute(rim, "dom", route)


def along_columns(rim, offset):
    route = [(i - offset, i) for i in range(PX * PY) if 0 <= i % PY - offset < PY]
    return lax.ppermute(rim, "dom", route)


def halo(low, high, front, back):
    from_low, from_high = along_rows(high, 1), along_rows(low, -1)
    from_front, from_back = along_columns(back, 1), along_columns(front, -1)
    side_shape = (CX, DEEP, GROUP, NZ)
    front_side = from_front[: CX * DEEP].reshape(side_shape)
    back_side = from_back[: CX * DEEP].reshape(side_shape)

    def corners(planes):
        return jnp.concatenate(
            (front_side[planes, DEEP - REACH :], back_side[planes, :REACH]), axis=1
        )

    low_corner = along_rows(corners(slice(CX - REACH, CX)), 1)
    high_corner = along_rows(corners(slice(0, REACH)), -1)
    return from_low, from_high, from_front, from_back, low_corner, high_corner


def filtered_halves(orbitals, potential):
    field = orbitals.transpose(1, 2, 0, 3)
    along = jnp.asarray(third_dimension_matrix())
    tiles = DEEP * CY
    block = (CX, CY, GROUP, NZ)
    wide = (CX + 2 * REACH, CY + 2 * REACH, GROUP, NZ)
    padded = (CX + 2 * DEEP, CY + 2 * DEEP, GROUP, NZ)
    rims = call(rims_kernel, [(tiles + 8, GROUP, NZ)] * 4, [], field, potential)
    once, twice, wide_potential, *rims = call(
        first_pair_kernel,
        [wide, block, wide[:2] + (NZ,)] + [(tiles, GROUP, NZ)] * 4,
        [padded],
        field, potential, *halo(*rims), along,
    )
    return call(
        second_pair_kernel,
        [(tiles, GROUP, NZ)] * 2,
        [padded, wide],
        twice, once, wide_potential, *halo(*rims), along,
    )


def over_y(block):
    return lax.all_to_all(block, "band", 0, 0, axis_index_groups=Y_RINGS, tiled=True)


def across(block):
    return lax.ppermute(block, "band", [(i, i ^ 1) for i in range(8)])


def small_exchange(chunks, groups):
    return lax.all_to_all(chunks, ("band", "dom"), 0, 0, axis_index_groups=groups, tiled=True)


def spread(row, groups):
    count = len(groups[0])
    return small_exchange(jnp.broadcast_to(row, (count,) + row.shape[1:]), groups)


def all_bands(mine, theirs, row, count, side):
    columns = []
    for offset in range(count):
        tiles = []
        for ring in range(4):
            own, other = mine[ring * HALF + row + offset], theirs[ring * HALF + row + offset]
            tiles += [jnp.where(side == 0, own, other), jnp.where(side == 0, other, own)]
        columns.append(jnp.concatenate(tiles, axis=0))
    return jnp.concatenate(columns, axis=1)


def gram_kernel(kept, taken, gram):
    side = lax.axis_index("band") % 2

    def body(step, total):
        bands = all_bands(kept, taken, step * 8, 8, side)
        return total + lax.dot_general(
            bands,
            bands,
            (((1,), (1,)), ((), ())),
            precision=lax.Precision.HIGHEST,
            preferred_element_type=jnp.float32,
        )

    total = lax.fori_loop(0, HALF // 8, body, jnp.zeros((BANDS, BANDS), jnp.float32))
    gram[...] = jnp.concatenate((total[: BANDS // 2], total[BANDS // 2 :]), axis=1)


def factor_kernel(cell_count, gram, inverse):
    both = gram[...] * (1.0 / cell_count)
    matrix = jnp.concatenate((both[:, :BANDS], both[:, BANDS:]), axis=0)
    rows = lax.broadcasted_iota(jnp.int32, (BANDS, BANDS), 0)
    columns = lax.broadcasted_iota(jnp.int32, (BANDS, BANDS), 1)
    work = jnp.concatenate((matrix, jnp.where(rows == columns, 1.0, 0.0)), axis=1)
    row_index = lax.broadcasted_iota(jnp.int32, (BANDS, 2 * BANDS), 0)
    scales = jnp.zeros((BANDS, 2 * BANDS), jnp.float32)
    for step in range(BANDS):
        pivot_row = work[step : step + 1]
        column = jnp.broadcast_to(work[:, step : step + 1], work.shape)
        pivot = jnp.broadcast_to(column[step : step + 1], work.shape)
        scales = jnp.where(row_index == step, pivot, scales)
        below = jnp.where(row_index > step, column / pivot, 0.0)
        work = work - below * pivot_row
    inverse[...] = (work * lax.rsqrt(scales))[:, BANDS:]


def rotation_kernel(inverse, kept, taken, given, late_0, late_1, late_2, rotated, taken_late):
    side = lax.axis_index("band") % 2
    place = 0
    for late in (late_0, late_1, late_2):
        taken_late[place : place + late.shape[0]] = late[...]
        place += late.shape[0]
    own = jnp.concatenate(
        [inverse[pl.ds(pl.multiple_of((2 * ring + side) * GROUP, GROUP), GROUP)] for ring in range(4)],
        axis=0,
    )
    for mine, theirs, half in ((kept, taken, side), (given, taken_late, 1 - side)):

        def body(step, carry, mine=mine, theirs=theirs, half=half):
            bands = all_bands(mine, theirs, step * 8, 8, side)
            turned = jnp.dot(
                own,
                bands,
                precision=lax.Precision.HIGHEST,
                preferred_element_type=jnp.float32,
            )
            for offset in range(8):
                for ring in range(4):
                    rotated[ring * 2 * HALF + half * HALF + step * 8 + offset] = turned[
                        ring * GROUP : (ring + 1) * GROUP, offset * NZ : (offset + 1) * NZ
                    ]
            return carry

        lax.fori_loop(0, HALF // 8, body, 0)


def on_device(orbitals, potential):
    cell_count = CX * CY * NZ * lax.axis_size("dom")
    given, kept = filtered_halves(orbitals[:, 0], potential[0])
    given = over_y(given)
    taken = across(given)
    kept = over_y(kept)
    kept, taken = lax.optimization_barrier((kept, taken))
    first, second, third = kept[:48], kept[48:88], kept[88:]
    late_0 = across(first)
    (gram,) = call(gram_kernel, [(32, 128)], [], kept, taken)
    row = small_exchange(gram[:, None], SHEETS).sum(axis=0, keepdims=True)
    row, late_0, second = lax.optimization_barrier((row, late_0, second))
    late_1 = across(second)
    row = spread(row, Z_RINGS).sum(axis=0, keepdims=True)
    row, late_1, third = lax.optimization_barrier((row, late_1, third))
    late_2 = across(third)
    gram = spread(row, SHEETS)[:, 0]
    (inverse,) = call(functools.partial(factor_kernel, cell_count), [(BANDS, BANDS)], [], gram)
    (rotated,) = call(
        rotation_kernel,
        [(CX * CY, GROUP, NZ)],
        [(4 * HALF, GROUP, NZ)],
        inverse, kept, taken, given, late_0, late_1, late_2,
    )
    rotated = over_y(rotated)
    return rotated.transpose(1, 0, 2).reshape(orbitals.shape)


def solution(mesh):
    placed = (P("band", "dom", None, None, None), P("dom", None, None, None))
    return jax.shard_map(
        on_device,
        mesh=mesh,
        in_specs=placed,
        out_specs=P("band", "dom", None, None, None),
        check_vma=False,
    )
```

```python
import functools

import functools

import jax
import jax.numpy as jnp
import numpy as np
from jax import lax
from jax.experimental import pallas as pl
from jax.experimental.pallas import tpu as pltpu
from jax.sharding import PartitionSpec as P

STENCIL = (-205.0 / 72.0, 8.0 / 5.0, -1.0 / 5.0, 8.0 / 315.0, -1.0 / 560.0)
FILTER_LOW = 1.5
FILTER_HIGH = 14.0
MIDDLE = 0.5 * (FILTER_HIGH + FILTER_LOW)
RADIUS = 0.5 * (FILTER_HIGH - FILTER_LOW)
SIDE_STEP = tuple(-0.5 * c / RADIUS for c in STENCIL)

PX = 8
PY = 8
CX = 16
CY = 16
NZ = 128
GROUP = 8
REACH = 4
DEEP = 8
BANDS = 64
HALF = 32
VMEM_BYTES = 40 * 2**20


def member(y, z_hi, z_lo, plane):
    return (y * 2 + z_hi) * 64 + z_lo * 8 + plane


Y_RINGS = [[0, 2, 4, 6], [1, 3, 5, 7]]
SHEETS = [
    [member(y, z_hi, z_lo, plane) for y in range(4) for plane in range(8)]
    for z_hi in range(2)
    for z_lo in range(8)
]
Z_RINGS = [
    [member(y, z_hi, z_lo, plane) for z_hi in range(2) for z_lo in range(8)]
    for y in range(4)
    for plane in range(8)
]


def third_dimension_matrix():
    matrix = np.zeros((NZ, NZ))
    for offset in range(1, REACH + 1):
        band = np.eye(NZ, k=offset) + np.eye(NZ, k=-offset)
        matrix += SIDE_STEP[offset] * band
    matrix += np.eye(NZ) * (3.0 * SIDE_STEP[0] - MIDDLE / RADIUS)
    return matrix.astype(np.float32)


def parts(matrix):
    high = matrix.astype(jnp.bfloat16)
    return high, (matrix - high.astype(jnp.float32)).astype(jnp.bfloat16)


def product(left, right, contract=(1, 0)):
    def one(a, b):
        return lax.dot_general(
            a, b, (((contract[0],), (contract[1],)), ((), ())), preferred_element_type=jnp.float32
        )

    (left_high, left_low), (right_high, right_low) = parts(left), parts(right)
    return one(left_high, right_high) + (one(left_low, right_high) + one(left_high, right_low))


def scaled_hamiltonian(field, potential, along, plane, first, count, origin):
    here = field[plane, pl.ds(first, count)]
    total = product(here.reshape(count * GROUP, NZ), along[...]).reshape(count, GROUP, NZ)
    for offset in range(1, REACH + 1):
        total += SIDE_STEP[offset] * (
            (field[plane + offset, pl.ds(first, count)] + field[plane - offset, pl.ds(first, count)])
            + (
                field[plane, pl.ds(first + offset, count)]
                + field[plane, pl.ds(first - offset, count)]
            )
        )
    local = potential[plane - origin, pl.ds(first - origin, count)] * (1.0 / RADIUS)
    return total + local[:, None, :] * here


def rims_kernel(field, potential, low, high, front, back):
    low[: DEEP * CY] = field[:DEEP].reshape(DEEP * CY, GROUP, NZ)
    high[: DEEP * CY] = field[CX - DEEP :].reshape(DEEP * CY, GROUP, NZ)
    front[: CX * DEEP] = field[:, :DEEP].reshape(CX * DEEP, GROUP, NZ)
    back[: CX * DEEP] = field[:, CY - DEEP :].reshape(CX * DEEP, GROUP, NZ)
    if potential is not None:
        tail = DEEP * CY
        low[tail:] = potential[:REACH].reshape(8, 8, NZ)
        high[tail:] = potential[CX - REACH :].reshape(8, 8, NZ)
        for plane in range(CX):
            slot, row = tail + plane // 2, plane % 2 * REACH
            front[slot, row : row + REACH] = potential[plane, :REACH]
            back[slot, row : row + REACH] = potential[plane, CY - REACH :]


def fill_padded(padded, field, low, high, front, back, low_corner, high_corner):
    end = DEEP + CX
    padded[DEEP:end, DEEP:end] = field[...]
    padded[:DEEP, DEEP:end] = low[: DEEP * CY].reshape(DEEP, CY, GROUP, NZ)
    padded[end:, DEEP:end] = high[: DEEP * CY].reshape(DEEP, CY, GROUP, NZ)
    padded[DEEP:end, :DEEP] = front[: CX * DEEP].reshape(CX, DEEP, GROUP, NZ)
    padded[DEEP:end, end:] = back[: CX * DEEP].reshape(CX, DEEP, GROUP, NZ)
    for rows, corner in ((DEEP - REACH, low_corner), (end, high_corner)):
        padded[rows : rows + REACH, DEEP - REACH : DEEP] = corner[:, :REACH]
        padded[rows : rows + REACH, end : end + REACH] = corner[:, REACH:]


def kept_sides():
    place = lax.axis_index("dom")
    row, column = place // PY, place % PY
    return tuple(
        jnp.where(edge, 0.0, 1.0)
        for edge in (row == 0, row == PX - 1, column == 0, column == PY - 1)
    )


def wide_step(padded, potential, along, earlier, later):
    keep_low, keep_high, keep_front, keep_back = kept_sides()

    def value(plane, first, count):
        total = scaled_hamiltonian(padded, potential, along, plane + DEEP, first + DEEP, count, REACH)
        if earlier is not None:
            total = 2.0 * total - earlier[plane + REACH, pl.ds(first + REACH, count)]
        return total

    def middle(plane, carry):
        total = value(plane, -REACH, CY + 2 * REACH)
        later[plane + REACH, :REACH] = total[:REACH] * keep_front
        later[plane + REACH, REACH : REACH + CY] = total[REACH : REACH + CY]
        later[plane + REACH, REACH + CY :] = total[REACH + CY :] * keep_back
        return carry

    def outer(layer, carry):
        later[layer, REACH : REACH + CY] = value(layer - REACH, 0, CY) * keep_low
        later[layer + CX + REACH, REACH : REACH + CY] = value(layer + CX, 0, CY) * keep_high
        return carry

    lax.fori_loop(0, CX, middle, 0, unroll=True)
    lax.fori_loop(0, REACH, outer, 0, unroll=True)


def narrow_step(wide, potential, along, earlier, store):
    def body(plane, carry):
        total = scaled_hamiltonian(wide, potential, along, plane + REACH, REACH, CY, 0)
        store(plane, 2.0 * total - earlier[plane])
        return carry

    lax.fori_loop(0, CX, body, 0, unroll=True)


def first_pair_kernel(
    field, potential, low, high, front, back, low_corner, high_corner, along,
    once, twice, wide_potential, next_low, next_high, next_front, next_back, padded,
):
    fill_padded(padded, field, low, high, front, back, low_corner, high_corner)
    tail, end = DEEP * CY, REACH + CX
    wide_potential[...] = jnp.zeros_like(wide_potential)
    wide_potential[REACH:end, REACH:end] = potential[...]
    wide_potential[:REACH, REACH:end] = low[tail:].reshape(REACH, CY, NZ)
    wide_potential[end:, REACH:end] = high[tail:].reshape(REACH, CY, NZ)
    for plane in range(CX):
        slot, row = tail + plane // 2, plane % 2 * REACH
        wide_potential[REACH + plane, :REACH] = front[slot, row : row + REACH]
        wide_potential[REACH + plane, end:] = back[slot, row : row + REACH]
    wide_step(padded, wide_potential, along, None, once)

    def store(plane, total):
        twice[plane] = total

    narrow_step(once, wide_potential, along, field, store)
    rims_kernel(twice, None, next_low, next_high, next_front, next_back)


def second_pair_kernel(
    field, once, potential, low, high, front, back, low_corner, high_corner, along,
    given, kept, padded, wide,
):
    fill_padded(padded, field, low, high, front, back, low_corner, high_corner)
    wide_step(padded, potential, along, once, wide)
    side = lax.axis_index("band") % 2

    def store(plane, total):
        row = pl.multiple_of((plane // 4 * 2 + plane % 2) * CY, CY)
        mine = plane // 2 % 2 == side

        @pl.when(mine)
        def _():
            kept[pl.ds(row, CY)] = total

        @pl.when(jnp.logical_not(mine))
        def _():
            given[pl.ds(row, CY)] = total

    narrow_step(wide, potential, along, field, store)


def call(kernel, shapes, scratch, *operands):
    whole = pl.BlockSpec(memory_space=pltpu.VMEM)
    return pl.pallas_call(
        kernel,
        out_shape=[jax.ShapeDtypeStruct(shape, jnp.float32) for shape in shapes],
        in_specs=[whole] * len(operands),
        out_specs=[whole] * len(shapes),
        scratch_shapes=[pltpu.VMEM(shape, jnp.float32) for shape in scratch],
        compiler_params=pltpu.CompilerParams(vmem_limit_bytes=VMEM_BYTES),
    )(*operands)


def along_rows(rim, offset):
    route = [(i - offset * PY, i) for i in range(PX * PY) if 0 <= i // PY - offset < PX]
    return lax.ppermute(rim, "dom", route)


def along_columns(rim, offset):
    route = [(i - offset, i) for i in range(PX * PY) if 0 <= i % PY - offset < PY]
    return lax.ppermute(rim, "dom", route)


def halo(low, high, front, back):
    from_low, from_high = along_rows(high, 1), along_rows(low, -1)
    from_front, from_back = along_columns(back, 1), along_columns(front, -1)
    side_shape = (CX, DEEP, GROUP, NZ)
    front_side = from_front[: CX * DEEP].reshape(side_shape)
    back_side = from_back[: CX * DEEP].reshape(side_shape)

    def corners(planes):
        return jnp.concatenate(
            (front_side[planes, DEEP - REACH :], back_side[planes, :REACH]), axis=1
        )

    low_corner = along_rows(corners(slice(CX - REACH, CX)), 1)
    high_corner = along_rows(corners(slice(0, REACH)), -1)
    return from_low, from_high, from_front, from_back, low_corner, high_corner


def filtered_halves(orbitals, potential):
    field = orbitals.transpose(1, 2, 0, 3)
    along = jnp.asarray(third_dimension_matrix())
    tiles = DEEP * CY
    block = (CX, CY, GROUP, NZ)
    wide = (CX + 2 * REACH, CY + 2 * REACH, GROUP, NZ)
    padded = (CX + 2 * DEEP, CY + 2 * DEEP, GROUP, NZ)
    rims = call(rims_kernel, [(tiles + 8, GROUP, NZ)] * 4, [], field, potential)
    once, twice, wide_potential, *rims = call(
        first_pair_kernel,
        [wide, block, wide[:2] + (NZ,)] + [(tiles, GROUP, NZ)] * 4,
        [padded],
        field, potential, *halo(*rims), along,
    )
    return call(
        second_pair_kernel,
        [(tiles, GROUP, NZ)] * 2,
        [padded, wide],
        twice, once, wide_potential, *halo(*rims), along,
    )


def over_y(block):
    return lax.all_to_all(block, "band", 0, 0, axis_index_groups=Y_RINGS, tiled=True)


def across(block):
    return lax.ppermute(block, "band", [(i, i ^ 1) for i in range(8)])


def small_exchange(chunks, groups):
    return lax.all_to_all(chunks, ("band", "dom"), 0, 0, axis_index_groups=groups, tiled=True)


def spread(row, groups):
    count = len(groups[0])
    return small_exchange(jnp.broadcast_to(row, (count,) + row.shape[1:]), groups)


def all_bands(mine, theirs, row, count, side):
    columns = []
    for offset in range(count):
        tiles = []
        for ring in range(4):
            own, other = mine[ring * HALF + row + offset], theirs[ring * HALF + row + offset]
            tiles += [jnp.where(side == 0, own, other), jnp.where(side == 0, other, own)]
        columns.append(jnp.concatenate(tiles, axis=0))
    return jnp.concatenate(columns, axis=1)


def gram_kernel(kept, taken, gram):
    side = lax.axis_index("band") % 2
    total = jnp.zeros((BANDS, BANDS), jnp.float32)
    for step in range(HALF // 8):
        bands = all_bands(kept, taken, step * 8, 8, side)
        total = total + product(bands, bands, (1, 1))
    gram[...] = jnp.concatenate((total[: BANDS // 2], total[BANDS // 2 :]), axis=1)


def factor_kernel(cell_count, gram, inverse):
    both = gram[...] * (1.0 / cell_count)
    matrix = jnp.concatenate((both[:, :BANDS], both[:, BANDS:]), axis=0)
    rows = lax.broadcasted_iota(jnp.int32, (BANDS, BANDS), 0)
    columns = lax.broadcasted_iota(jnp.int32, (BANDS, BANDS), 1)
    work = jnp.concatenate((matrix, jnp.where(rows == columns, 1.0, 0.0)), axis=1)
    row_index = lax.broadcasted_iota(jnp.int32, (BANDS, 2 * BANDS), 0)
    scales = jnp.zeros((BANDS, 2 * BANDS), jnp.float32)
    for step in range(BANDS):
        pivot_row = work[step : step + 1]
        column = jnp.broadcast_to(work[:, step : step + 1], work.shape)
        pivot = jnp.broadcast_to(column[step : step + 1], work.shape)
        scales = jnp.where(row_index == step, pivot, scales)
        below = jnp.where(row_index > step, column / pivot, 0.0)
        work = work - below * pivot_row
    inverse[...] = (work * lax.rsqrt(scales))[:, BANDS:]


def rotation_kernel(inverse, mine, *rest):
    theirs, rotated = rest[:-1], rest[-1]
    if len(theirs) > 1:
        *pieces, rotated, theirs = rest
        place = 0
        for piece in pieces:
            theirs[place : place + piece.shape[0]] = piece[...]
            place += piece.shape[0]
    else:
        theirs = theirs[0]
    side = lax.axis_index("band") % 2
    own = jnp.concatenate(
        [inverse[pl.ds(pl.multiple_of((2 * ring + side) * GROUP, GROUP), GROUP)] for ring in range(4)],
        axis=0,
    )
    for step in range(HALF // 8):
        bands = all_bands(mine, theirs, step * 8, 8, side)
        turned = product(own, bands)
        for offset in range(8):
            for ring in range(4):
                rotated[ring * HALF + step * 8 + offset] = turned[
                    ring * GROUP : (ring + 1) * GROUP, offset * NZ : (offset + 1) * NZ
                ]


def placing_kernel(early, late, rotated):
    side = lax.axis_index("band") % 2
    for quarter in range(4):
        for half in range(2):
            for step in range(HALF // 8):
                rows = pl.ds(quarter * HALF + step * 8, 8)
                tiles = jnp.where(side == half, early[rows], late[rows])
                place = (quarter * 2 + half) * HALF + step * 8
                rotated[:, place : place + 8] = jnp.swapaxes(tiles, 0, 1)


def on_device(orbitals, potential):
    cell_count = CX * CY * NZ * lax.axis_size("dom")
    given, kept = filtered_halves(orbitals[:, 0], potential[0])
    given = over_y(given)
    taken = across(given)
    kept = over_y(kept)
    kept, taken = lax.optimization_barrier((kept, taken))
    first, second, third, fourth = kept[:40], kept[40:72], kept[72:96], kept[96:]
    late_0 = across(first)
    (gram,) = call(gram_kernel, [(32, 128)], [], kept, taken)
    row = small_exchange(gram[:, None], SHEETS).sum(axis=0, keepdims=True)
    row, late_0, second = lax.optimization_barrier((row, late_0, second))
    row = spread(row, Z_RINGS).sum(axis=0, keepdims=True)
    row, second = lax.optimization_barrier((row, second))
    late_1 = across(second)
    gram = spread(row, SHEETS)[:, 0]
    gram, late_1, third = lax.optimization_barrier((gram, late_1, third))
    late_2 = across(third)
    (inverse,) = call(functools.partial(factor_kernel, cell_count), [(BANDS, BANDS)], [], gram)
    tiles = (4 * HALF, GROUP, NZ)
    inverse, late_2, fourth = lax.optimization_barrier((inverse, late_2, fourth))
    late_3 = across(fourth)
    (early,) = call(rotation_kernel, [tiles], [], inverse, kept, taken)
    early = over_y(early)
    early, late_3 = lax.optimization_barrier((early, late_3))
    (late,) = call(
        rotation_kernel, [tiles], [tiles], inverse, given, late_0, late_1, late_2, late_3
    )
    late = over_y(late)
    (rotated,) = call(placing_kernel, [(GROUP, CX * CY, NZ)], [], early, late)
    return rotated.reshape(orbitals.shape)


def solution(mesh):
    placed = (P("band", "dom", None, None, None), P("dom", None, None, None))
    return jax.shard_map(
        on_device,
        mesh=mesh,
        in_specs=placed,
        out_specs=P("band", "dom", None, None, None),
        check_vma=False,
    )
```

```python
import functools

import functools

import jax
import jax.numpy as jnp
import numpy as np
from jax import lax
from jax.experimental import pallas as pl
from jax.experimental.pallas import tpu as pltpu
from jax.sharding import PartitionSpec as P

STENCIL = (-205.0 / 72.0, 8.0 / 5.0, -1.0 / 5.0, 8.0 / 315.0, -1.0 / 560.0)
FILTER_LOW = 1.5
FILTER_HIGH = 14.0
MIDDLE = 0.5 * (FILTER_HIGH + FILTER_LOW)
RADIUS = 0.5 * (FILTER_HIGH - FILTER_LOW)
SIDE_STEP = tuple(-0.5 * c / RADIUS for c in STENCIL)

PX = 8
PY = 8
CX = 16
CY = 16
NZ = 128
GROUP = 8
REACH = 4
DEEP = 8
BANDS = 64
HALF = 32
PIVOTS = 4
VMEM_BYTES = 40 * 2**20


def member(y, z_hi, z_lo, plane):
    return (y * 2 + z_hi) * 64 + z_lo * 8 + plane


Y_RINGS = [[0, 2, 4, 6], [1, 3, 5, 7]]
Z_PAIRS = [[0, 1], [2, 3], [4, 5], [6, 7]]
SHEETS = [
    [member(y, z_hi, z_lo, plane) for y in range(4) for plane in range(8)]
    for z_hi in range(2)
    for z_lo in range(8)
]
Z_RINGS = [
    [member(y, z_hi, z_lo, plane) for z_hi in range(2) for z_lo in range(8)]
    for y in range(4)
    for plane in range(8)
]


def third_dimension_matrix():
    matrix = np.zeros((NZ, NZ))
    for offset in range(1, REACH + 1):
        band = np.eye(NZ, k=offset) + np.eye(NZ, k=-offset)
        matrix += SIDE_STEP[offset] * band
    matrix += np.eye(NZ) * (3.0 * SIDE_STEP[0] - MIDDLE / RADIUS)
    return matrix.astype(np.float32)


def parts(matrix):
    high = matrix.astype(jnp.bfloat16)
    return high, (matrix - high.astype(jnp.float32)).astype(jnp.bfloat16)


def product(left, right, contract=(1, 0)):
    def one(a, b):
        return lax.dot_general(
            a, b, (((contract[0],), (contract[1],)), ((), ())), preferred_element_type=jnp.float32
        )

    (left_high, left_low), (right_high, right_low) = parts(left), parts(right)
    return one(left_high, right_high) + (one(left_low, right_high) + one(left_high, right_low))


def scaled_hamiltonian(field, potential, along, plane, first, count, origin):
    here = field[plane, pl.ds(first, count)]
    total = product(here.reshape(count * GROUP, NZ), along[...]).reshape(count, GROUP, NZ)
    for offset in range(1, REACH + 1):
        total += SIDE_STEP[offset] * (
            (field[plane + offset, pl.ds(first, count)] + field[plane - offset, pl.ds(first, count)])
            + (
                field[plane, pl.ds(first + offset, count)]
                + field[plane, pl.ds(first - offset, count)]
            )
        )
    local = potential[plane - origin, pl.ds(first - origin, count)] * (1.0 / RADIUS)
    return total + local[:, None, :] * here


def rims_kernel(field, potential, low, high, front, back):
    low[: DEEP * CY] = field[:DEEP].reshape(DEEP * CY, GROUP, NZ)
    high[: DEEP * CY] = field[CX - DEEP :].reshape(DEEP * CY, GROUP, NZ)
    front[: CX * DEEP] = field[:, :DEEP].reshape(CX * DEEP, GROUP, NZ)
    back[: CX * DEEP] = field[:, CY - DEEP :].reshape(CX * DEEP, GROUP, NZ)
    if potential is not None:
        tail = DEEP * CY
        low[tail:] = potential[:REACH].reshape(8, 8, NZ)
        high[tail:] = potential[CX - REACH :].reshape(8, 8, NZ)
        for plane in range(CX):
            slot, row = tail + plane // 2, plane % 2 * REACH
            front[slot, row : row + REACH] = potential[plane, :REACH]
            back[slot, row : row + REACH] = potential[plane, CY - REACH :]


def fill_padded(padded, field, low, high, front, back, low_corner, high_corner):
    end = DEEP + CX
    padded[DEEP:end, DEEP:end] = field[...]
    padded[:DEEP, DEEP:end] = low[: DEEP * CY].reshape(DEEP, CY, GROUP, NZ)
    padded[end:, DEEP:end] = high[: DEEP * CY].reshape(DEEP, CY, GROUP, NZ)
    padded[DEEP:end, :DEEP] = front[: CX * DEEP].reshape(CX, DEEP, GROUP, NZ)
    padded[DEEP:end, end:] = back[: CX * DEEP].reshape(CX, DEEP, GROUP, NZ)
    for rows, corner in ((DEEP - REACH, low_corner), (end, high_corner)):
        padded[rows : rows + REACH, DEEP - REACH : DEEP] = corner[:, :REACH]
        padded[rows : rows + REACH, end : end + REACH] = corner[:, REACH:]


def kept_sides():
    place = lax.axis_index("dom")
    row, column = place // PY, place % PY
    return tuple(
        jnp.where(edge, 0.0, 1.0)
        for edge in (row == 0, row == PX - 1, column == 0, column == PY - 1)
    )


def wide_step(padded, potential, along, earlier, later):
    keep_low, keep_high, keep_front, keep_back = kept_sides()

    def value(plane, first, count):
        total = scaled_hamiltonian(padded, potential, along, plane + DEEP, first + DEEP, count, REACH)
        if earlier is not None:
            total = 2.0 * total - earlier[plane + REACH, pl.ds(first + REACH, count)]
        return total

    def middle(plane, carry):
        total = value(plane, -REACH, CY + 2 * REACH)
        later[plane + REACH, :REACH] = total[:REACH] * keep_front
        later[plane + REACH, REACH : REACH + CY] = total[REACH : REACH + CY]
        later[plane + REACH, REACH + CY :] = total[REACH + CY :] * keep_back
        return carry

    def outer(layer, carry):
        later[layer, REACH : REACH + CY] = value(layer - REACH, 0, CY) * keep_low
        later[layer + CX + REACH, REACH : REACH + CY] = value(layer + CX, 0, CY) * keep_high
        return carry

    lax.fori_loop(0, CX, middle, 0, unroll=True)
    lax.fori_loop(0, REACH, outer, 0, unroll=True)


def narrow_step(wide, potential, along, earlier, store):
    def body(plane, carry):
        total = scaled_hamiltonian(wide, potential, along, plane + REACH, REACH, CY, 0)
        store(plane, 2.0 * total - earlier[plane])
        return carry

    lax.fori_loop(0, CX, body, 0, unroll=True)


def first_pair_kernel(
    field, potential, low, high, front, back, low_corner, high_corner, along,
    once, twice, wide_potential, next_low, next_high, next_front, next_back, padded,
):
    fill_padded(padded, field, low, high, front, back, low_corner, high_corner)
    tail, end = DEEP * CY, REACH + CX
    wide_potential[...] = jnp.zeros_like(wide_potential)
    wide_potential[REACH:end, REACH:end] = potential[...]
    wide_potential[:REACH, REACH:end] = low[tail:].reshape(REACH, CY, NZ)
    wide_potential[end:, REACH:end] = high[tail:].reshape(REACH, CY, NZ)
    for plane in range(CX):
        slot, row = tail + plane // 2, plane % 2 * REACH
        wide_potential[REACH + plane, :REACH] = front[slot, row : row + REACH]
        wide_potential[REACH + plane, end:] = back[slot, row : row + REACH]
    wide_step(padded, wide_potential, along, None, once)

    def store(plane, total):
        twice[plane] = total

    narrow_step(once, wide_potential, along, field, store)
    rims_kernel(twice, None, next_low, next_high, next_front, next_back)


def second_pair_kernel(
    field, once, potential, low, high, front, back, low_corner, high_corner, along,
    given, kept, padded, wide,
):
    fill_padded(padded, field, low, high, front, back, low_corner, high_corner)
    wide_step(padded, potential, along, once, wide)
    side = lax.axis_index("band") % 2

    def store(plane, total):
        row = pl.multiple_of((plane // 4 * 2 + plane % 2) * CY, CY)
        mine = plane // 2 % 2 == side

        @pl.when(mine)
        def _():
            kept[pl.ds(row, CY)] = total

        @pl.when(jnp.logical_not(mine))
        def _():
            given[pl.ds(row, CY)] = total

    narrow_step(wide, potential, along, field, store)


def call(kernel, shapes, scratch, *operands):
    whole = pl.BlockSpec(memory_space=pltpu.VMEM)
    return pl.pallas_call(
        kernel,
        out_shape=[jax.ShapeDtypeStruct(shape, jnp.float32) for shape in shapes],
        in_specs=[whole] * len(operands),
        out_specs=[whole] * len(shapes),
        scratch_shapes=[pltpu.VMEM(shape, jnp.float32) for shape in scratch],
        compiler_params=pltpu.CompilerParams(vmem_limit_bytes=VMEM_BYTES),
    )(*operands)


def along_rows(rim, offset):
    route = [(i - offset * PY, i) for i in range(PX * PY) if 0 <= i // PY - offset < PX]
    return lax.ppermute(rim, "dom", route)


def along_columns(rim, offset):
    route = [(i - offset, i) for i in range(PX * PY) if 0 <= i % PY - offset < PY]
    return lax.ppermute(rim, "dom", route)


def halo(low, high, front, back):
    from_low, from_high = along_rows(high, 1), along_rows(low, -1)
    from_front, from_back = along_columns(back, 1), along_columns(front, -1)
    side_shape = (CX, DEEP, GROUP, NZ)
    front_side = from_front[: CX * DEEP].reshape(side_shape)
    back_side = from_back[: CX * DEEP].reshape(side_shape)

    def corners(planes):
        return jnp.concatenate(
            (front_side[planes, DEEP - REACH :], back_side[planes, :REACH]), axis=1
        )

    low_corner = along_rows(corners(slice(CX - REACH, CX)), 1)
    high_corner = along_rows(corners(slice(0, REACH)), -1)
    return from_low, from_high, from_front, from_back, low_corner, high_corner


def filtered_halves(orbitals, potential):
    field = orbitals.transpose(1, 2, 0, 3)
    along = jnp.asarray(third_dimension_matrix())
    tiles = DEEP * CY
    block = (CX, CY, GROUP, NZ)
    wide = (CX + 2 * REACH, CY + 2 * REACH, GROUP, NZ)
    padded = (CX + 2 * DEEP, CY + 2 * DEEP, GROUP, NZ)
    rims = call(rims_kernel, [(tiles + 8, GROUP, NZ)] * 4, [], field, potential)
    once, twice, wide_potential, *rims = call(
        first_pair_kernel,
        [wide, block, wide[:2] + (NZ,)] + [(tiles, GROUP, NZ)] * 4,
        [padded],
        field, potential, *halo(*rims), along,
    )
    return call(
        second_pair_kernel,
        [(tiles, GROUP, NZ)] * 2,
        [padded, wide],
        twice, once, wide_potential, *halo(*rims), along,
    )


def over_y(block):
    return lax.all_to_all(block, "band", 0, 0, axis_index_groups=Y_RINGS, tiled=True)


def across(block):
    return lax.ppermute(block, "band", [(i, i ^ 1) for i in range(8)])


def small_exchange(chunks, groups):
    return lax.all_to_all(chunks, ("band", "dom"), 0, 0, axis_index_groups=groups, tiled=True)


def spread(row, groups):
    count = len(groups[0])
    return small_exchange(jnp.broadcast_to(row, (count,) + row.shape[1:]), groups)


def all_bands(mine, theirs, row, count, side):
    columns = []
    for offset in range(count):
        tiles = []
        for ring in range(4):
            own, other = mine[ring * HALF + row + offset], theirs[ring * HALF + row + offset]
            tiles += [jnp.where(side == 0, own, other), jnp.where(side == 0, other, own)]
        columns.append(jnp.concatenate(tiles, axis=0))
    return jnp.concatenate(columns, axis=1)


def gram_kernel(kept, taken, gram):
    side = lax.axis_index("band") % 2
    total = jnp.zeros((BANDS, BANDS), jnp.float32)
    for step in range(HALF // 8):
        bands = all_bands(kept, taken, step * 8, 8, side)
        total = total + product(bands, bands, (1, 1))
    gram[...] = jnp.concatenate((total[: BANDS // 2], total[BANDS // 2 :]), axis=1)


def factor_kernel(cell_count, gram, inverse):
    both = gram[...] * (1.0 / cell_count)
    matrix = jnp.concatenate((both[:, :BANDS], both[:, BANDS:]), axis=0)
    rows = lax.broadcasted_iota(jnp.int32, (BANDS, BANDS), 0)
    columns = lax.broadcasted_iota(jnp.int32, (BANDS, BANDS), 1)
    work = jnp.concatenate((jnp.where(rows == columns, 1.0, 0.0), matrix), axis=1)
    row_index = lax.broadcasted_iota(jnp.int32, work.shape, 0)
    for start in range(0, BANDS, PIVOTS):
        picked = [
            jnp.broadcast_to(work[:, BANDS + step : BANDS + step + 1], work.shape)
            for step in range(start, start + PIVOTS)
        ]
        pivot_rows = [work[step : step + 1] for step in range(start, start + PIVOTS)]
        for j in range(PIVOTS):
            here = slice(start + j, start + j + 1)
            pivot = picked[j][here]
            below = jnp.where(row_index > start + j, picked[j] * (1.0 / pivot), 0.0)
            for later in range(j + 1, PIVOTS):
                there = slice(start + later, start + later + 1)
                picked[later] = picked[later] - below * picked[later][here]
                pivot_rows[later] = pivot_rows[later] - below[there] * pivot_rows[j]
            work = work - below * pivot_rows[j]
            inverse[here] = (pivot_rows[j] * lax.rsqrt(pivot))[:, :BANDS]


def rotation_kernel(inverse, mine, theirs, rotated):
    side = lax.axis_index("band") % 2
    if len(theirs.shape) == 4:
        theirs = theirs.at[1 - side]
    own = jnp.concatenate(
        [inverse[pl.ds(pl.multiple_of((2 * ring + side) * GROUP, GROUP), GROUP)] for ring in range(4)],
        axis=0,
    )
    for step in range(HALF // 8):
        bands = all_bands(mine, theirs, step * 8, 8, side)
        turned = product(own, bands)
        for offset in range(8):
            for ring in range(4):
                rotated[ring * HALF + step * 8 + offset] = turned[
                    ring * GROUP : (ring + 1) * GROUP, offset * NZ : (offset + 1) * NZ
                ]


def placing_kernel(early, late, rotated):
    side = lax.axis_index("band") % 2
    for quarter in range(4):
        for half in range(2):
            for step in range(HALF // 8):
                rows = pl.ds(quarter * HALF + step * 8, 8)
                tiles = jnp.where(side == half, early[rows], late[rows])
                place = (quarter * 2 + half) * HALF + step * 8
                rotated[:, place : place + 8] = jnp.swapaxes(tiles, 0, 1)


def on_device(orbitals, potential):
    cell_count = CX * CY * NZ * lax.axis_size("dom")
    given, kept = filtered_halves(orbitals[:, 0], potential[0])
    given = over_y(given)
    taken = across(given)
    kept = over_y(kept)
    kept, taken = lax.optimization_barrier((kept, taken))
    pair = lax.all_gather(kept, "band", axis=0, axis_index_groups=Z_PAIRS)
    tiles = (4 * HALF, GROUP, NZ)

    def sum_factor_rotate(_, carry):
        (gram,) = call(gram_kernel, [(32, 128)], [], kept, taken)
        row = small_exchange(gram[:, None], SHEETS).sum(axis=0, keepdims=True)
        row = spread(row, Z_RINGS).sum(axis=0, keepdims=True)
        gram = spread(row, SHEETS)[:, 0]
        (inverse,) = call(functools.partial(factor_kernel, cell_count), [(BANDS, BANDS)], [], gram)
        (early,) = call(rotation_kernel, [tiles], [], inverse, kept, taken)
        return inverse, over_y(early)

    once = jnp.where(lax.axis_index("dom") < PX * PY, 1, 2)
    empty = (jnp.zeros((BANDS, BANDS), jnp.float32), jnp.zeros(tiles, jnp.float32))
    inverse, early = lax.fori_loop(0, once, sum_factor_rotate, empty)
    early, pair = lax.optimization_barrier((early, pair))
    (late,) = call(rotation_kernel, [tiles], [], inverse, given, pair)
    late = over_y(late)
    (rotated,) = call(placing_kernel, [(GROUP, CX * CY, NZ)], [], early, late)
    return rotated.reshape(orbitals.shape)


def solution(mesh):
    placed = (P("band", "dom", None, None, None), P("dom", None, None, None))
    return jax.shard_map(
        on_device,
        mesh=mesh,
        in_specs=placed,
        out_specs=P("band", "dom", None, None, None),
        check_vma=False,
    )
```
